128 devices in a mesh: swath: 8 (over y, core), seg: 16 (over z, x).
Axes of the slice: x: 4, y: 4, z: 4, core: 2. Of those that a mesh axis runs over, the one named last changes fastest.
Arguments:
- swath_pixels: bfloat16 [8, 16, 128, 1024], P('swath', 'seg'), may hold values from -6 to 6
- stencils: float32 [8, 2, 9], replicated, may hold values from -6 to 6
- classes: int32 [16, 16, 32], P('seg', 'swath'), may hold values from 0 to 7
- neighbours: int32 [16, 16, 2], P('seg'), may hold values from 0 to 15, as said below
Outputs:
- responses: bfloat16 [16, 4, 8, 128, 1024], P('seg', None, None, 'swath')
The draws below stay inside these ranges and needn't reach their ends.
Inputs may be any that keep to these rules, and one draw needn't show every extreme that they name: `neighbours`: the two entries of a row block of die j are different dies, each other than j.
All inputs are finite; a program needn't handle non-finite values.
Results may differ from the reference program's by a relative error of at most 0.0049.
Values may be sent and summed in bfloat16 or wider, within the bound.
No kernel may reach another device: no remote copies, remote signals or barrier semaphores. Data moves between devices by JAX's collectives and lax.ppermute only.
A program may use at most 64 MiB of HBM per device.

```python
import jax
import jax.numpy as jnp
from jax import lax

ROWS = 128
COLS = 512
CH = 2
BLK_R = 8
BLK_C = 128
NCLASS = 8
SWATHS = 8
DIES = 16


def draw_neighbours(key, part):
    blocks = ROWS // BLK_R
    key_one = jax.random.fold_in(key, 11)
    key_two = jax.random.fold_in(key, 23)
    first_step = jax.random.randint(key_one, (DIES, blocks), 1, DIES)
    second_step = jax.random.randint(key_two, (DIES, blocks), 1, DIES - 1)
    second_step = second_step + (second_step >= first_step).astype(jnp.int32)
    own_die = jnp.arange(DIES, dtype=jnp.int32)[:, None]
    first_die = (own_die + first_step) % DIES
    second_die = (own_die + second_step) % DIES
    return jnp.stack([first_die, second_die], axis=2).astype(jnp.int32)


def set_ends(result, key, low, high):
    longest = result.shape.index(max(result.shape))
    spots = []
    for shift in (0, 1):
        where = [jax.random.randint(jax.random.fold_in(key, axis), (), 0, length) for axis, length in enumerate(result.shape)]
        where[longest] = (where[longest] + shift) % result.shape[longest]
        spots.append(tuple(where))
    return result.at[spots[0]].set(low).at[spots[1]].set(high)


def levels(key, shape, shards, least, largest):
    factor_of, own = 1.0, jax.random.fold_in(key, 6)
    for axis_at, blocks in shards:
        heights = jnp.exp(jax.random.uniform(jax.random.fold_in(own, axis_at), (blocks,), jnp.float32, least / len(shards), largest / len(shards)))
        factor_of = factor_of * jnp.repeat(heights, shape[axis_at] // blocks).reshape([-1 if axis == axis_at else 1 for axis in range(len(shape))])
    return factor_of


def centred(rng, dims, scale, reach, cuts=(), kind=jnp.bfloat16):
    factor_of = levels(rng, dims, cuts, -0.22, 0.18) if cuts else 1.0
    entries = jax.random.normal(rng, dims, jnp.float32) * scale * factor_of
    return jnp.minimum(jnp.maximum(entries, -reach), reach).astype(kind)


def setup_inputs(seed: int = 0) -> dict:
    key_list = jax.random.split(jax.random.key(seed), 5)
    swath_pixels = centred(key_list[0], (SWATHS, DIES, ROWS, CH * COLS), 1.0, 6.0, ((0, 8), (1, 16)))
    stencils = centred(key_list[1], (NCLASS, CH, 9), 0.4, 6.0, (), jnp.float32)
    classes = set_ends(jax.random.randint(key_list[2], (DIES, ROWS // BLK_R, SWATHS * COLS // BLK_C), 0, NCLASS), jax.random.fold_in(key_list[2], 1), 0, NCLASS - 1).astype(jnp.int32)
    neighbours = draw_neighbours(jax.random.fold_in(key_list[4], 71), 0)
    return {"swath_pixels": swath_pixels, "stencils": stencils, "classes": classes, "neighbours": neighbours}


TAPS = (-0.5, 0.25, 1.0, 0.25, -0.5)
DIRECTIONS = ((0, 1), (1, 0), (1, 1), (1, -1))


def reference(swath_pixels, stencils, classes, neighbours):
    swaths, dies, rows_all, wide = swath_pixels.shape
    width = wide // CH
    across = swaths * width
    image = swath_pixels.reshape(swaths, dies, rows_all, CH, width).transpose(1, 3, 2, 0, 4).reshape(dies, CH, rows_all, across)

    def normalize(pieces):
        picture, class_map = pieces
        coef_map = stencils[class_map]
        padded = jnp.pad(picture.astype(jnp.float32), ((0, 0), (1, 1), (1, 1)))
        summed = jnp.zeros((CH, rows_all, across), jnp.float32)
        for step_row in (-1, 0, 1):
            for step_col in (-1, 0, 1):
                which = 3 * (step_row + 1) + step_col + 1
                spread = jnp.repeat(jnp.repeat(coef_map[..., which].transpose(2, 0, 1), BLK_R, axis=1), BLK_C, axis=2)
                summed = summed + spread * padded[:, 1 + step_row:1 + step_row + rows_all, 1 + step_col:1 + step_col + across]
        return summed.astype(jnp.bfloat16)

    normed = lax.map(normalize, (image, classes))
    row_ids = jnp.arange(rows_all)

    def respond(pieces):
        own, near = pieces
        picks = jnp.repeat(near, BLK_R, axis=0)
        filtered = []
        for which in range(2):
            other = normed[picks[:, which], :, row_ids, :].transpose(1, 0, 2)
            differ = own.astype(jnp.float32) - other.astype(jnp.float32)
            padded = jnp.pad(differ, ((0, 0), (2, 2), (2, 2)))
            per_dir = []
            for row_step, col_step in DIRECTIONS:
                response = 0.0
                for offset, weight in zip(range(-2, 3), TAPS):
                    start_row = 2 + row_step * offset
                    start_col = 2 + col_step * offset
                    response = response + weight * padded[:, start_row:start_row + rows_all, start_col:start_col + across]
                per_dir.append(response)
            filtered.append(jnp.stack(per_dir))
        lowest = jnp.minimum(filtered[0], filtered[1])
        lowest = lowest.reshape(4, CH, rows_all, swaths, width).transpose(0, 3, 2, 1, 4)
        return lowest.reshape(4, swaths, rows_all, CH * width).astype(jnp.bfloat16)

    return lax.map(respond, (normed, neighbours))
```

```python
import functools

import jax
import jax.numpy as jnp
from jax import lax
from jax.experimental import pallas as pl
from jax.experimental.pallas import tpu as pltpu
from jax.sharding import PartitionSpec as P

CH = 2
BLK_R = 8
BLK_C = 128
NCLASS = 8
SWATHS = 8
DIES = 16
ROWS = 128
COLS = 512
BAND = 16
PARTS = 16
COL_BLOCKS = SWATHS * COLS // BLK_C
WIDE = SWATHS * COLS + 2 * BLK_C
PIECE = COLS + BLK_C
VMEM_LIMIT = 24 * 1024 * 1024

TAPS = (-0.5, 0.25, 1.0, 0.25, -0.5)


def rows_of(count, width):
    return lax.broadcasted_iota(jnp.int32, (count, width), 0)


def pack_kernel(pix_ref, cls_ref, out_ref, row_ref):
    row_ref[...] = jnp.zeros_like(row_ref)
    row_ref[6:8, 0:COL_BLOCKS] = cls_ref[...].astype(jnp.float32)
    own_classes = row_ref[...]
    sub = rows_of(8, COLS)
    for band in range(SWATHS):
        start = band * BAND
        out_ref[band, :, 0 : CH * COLS] = pix_ref[start : start + BAND, :]
        for h in range(CH):
            lanes = slice(h * COLS, (h + 1) * COLS)
            if band > 0:
                above = pix_ref[start - BAND : start, lanes].astype(jnp.float32)[8:16]
                above = pltpu.roll(above, 3, 0)
            else:
                above = jnp.zeros((8, COLS), jnp.float32)
            if band < SWATHS - 1:
                below = pix_ref[start + BAND : start + 2 * BAND, lanes].astype(jnp.float32)[0:8]
                below = pltpu.roll(below, 3, 0)
            else:
                below = jnp.zeros((8, COLS), jnp.float32)
            halo = jnp.where(sub < 3, above, jnp.where(sub < 6, below, own_classes))
            if h == 0:
                first = halo
        out_ref[band, :, CH * COLS :] = jnp.concatenate([first, halo], axis=0).astype(jnp.bfloat16)


def norm_kernel(band, recv_ref, sten_ref, out_ref, image_ref, cls_v, cls_s, sem):
    if band is None:
        band = lax.axis_index("swath")
    before = jnp.maximum(band - 1, 0)
    after = jnp.minimum(band + 1, SWATHS - 1)

    def class_rows(source):
        return recv_ref[source, :, CH * COLS : CH * COLS + BLK_C].astype(jnp.float32)[0:8].astype(jnp.int32)

    cls_v[0:8] = class_rows(before)
    cls_v[8:16] = class_rows(band)
    cls_v[16:24] = class_rows(after)
    copy = pltpu.make_async_copy(cls_v, cls_s, sem)
    copy.start()

    for h in range(CH):
        image_ref[h, :, 0:BLK_C] = jnp.zeros((24, BLK_C), jnp.float32)
        image_ref[h, :, WIDE - BLK_C : WIDE] = jnp.zeros((24, BLK_C), jnp.float32)
        for g in range(SWATHS):
            lanes = slice(BLK_C + g * COLS, BLK_C + (g + 1) * COLS)
            image_ref[h, 0:16, lanes] = recv_ref[g, :, h * COLS : (h + 1) * COLS].astype(jnp.float32)
            halo = recv_ref[g, :, CH * COLS :].astype(jnp.float32)[h * 8 : h * 8 + 8]
            image_ref[h, 16:24, lanes] = pltpu.roll(halo, 5, 0)
    copy.wait()

    top = jnp.where(band > 0, 1.0, 0.0)
    bottom = jnp.where(band < SWATHS - 1, 1.0, 0.0)
    sub = rows_of(8, BLK_C)

    def step(g, carry):
        for h in range(CH):
            base = pl.multiple_of(g * COLS, COLS)
            window = image_ref[h, :, pl.ds(base, COLS + 2 * BLK_C)]
            wide = COLS + 2 * BLK_C
            cols = [
                pltpu.roll(window, 1, 1)[:, BLK_C : BLK_C + COLS],
                window[:, BLK_C : BLK_C + COLS],
                pltpu.roll(window, wide - 1, 1)[:, BLK_C : BLK_C + COLS],
            ]
            shifted = [[pltpu.roll(c, 1, 0), c, pltpu.roll(c, 23, 0)] for c in cols]
            above = jnp.zeros((8, BLK_C), jnp.float32)
            below = jnp.zeros((8, BLK_C), jnp.float32)
            for q in range(COLS // BLK_C):
                block = g * (COLS // BLK_C) + q
                offsets = [
                    (cls_s[row, block] * CH + h) * 9 for row in (7, 14, 15, 22)
                ]
                total = [jnp.zeros((8, BLK_C), jnp.float32) for _ in range(3)]
                lanes = slice(q * BLK_C, (q + 1) * BLK_C)
                for dr in range(3):
                    for dc in range(3):
                        k = 3 * dr + dc
                        coefs = [sten_ref[offset + k] for offset in offsets]
                        source = shifted[dc][dr]
                        edge = jnp.where(sub < 4, coefs[3] * bottom, coefs[0] * top)
                        total[0] = total[0] + coefs[1] * source[0:8, lanes]
                        total[1] = total[1] + coefs[2] * source[8:16, lanes]
                        total[2] = total[2] + edge * source[16:24, lanes]
                out_ref[2 * g + h, :, lanes] = jnp.concatenate(total[:2], axis=0).astype(jnp.bfloat16)
                mine = (sub // 2) == q
                above = jnp.where(mine, pltpu.roll(total[2], (2 * q + 2) % 8, 0), above)
                below = jnp.where(mine, pltpu.roll(total[2], 2 * q, 0) if q else total[2], below)
            out_ref[2 * g + h, :, COLS:] = jnp.concatenate([above, below], axis=0).astype(jnp.bfloat16)
        return carry

    lax.fori_loop(0, SWATHS, step, 0)


def pick_kernel(band, near_ref, recv_ref, out_ref):
    if band is None:
        band = lax.axis_index("swath")
    blocks = ROWS // BLK_R
    first = band * 2
    rows = (jnp.maximum(first - 1, 0), first, first + 1, jnp.minimum(first + 2, blocks - 1))
    main_top = rows_of(16, COLS) < 8
    edge_top = rows_of(16, BLK_C) < 8
    for die in range(DIES):
        for k in range(2):
            up, one, two, down = [near_ref[(die * blocks + row) * 2 + k] for row in rows]
            out_ref[2 * die + k, :, 0:COLS] = jnp.where(
                main_top, recv_ref[one, :, 0:COLS], recv_ref[two, :, 0:COLS]
            )
            out_ref[2 * die + k, :, COLS:] = jnp.where(
                edge_top, recv_ref[up, :, COLS:], recv_ref[down, :, COLS:]
            )


def unpack_edge(edge):
    sub = rows_of(8, BLK_C)
    tiles = []
    for q in range(COLS // BLK_C):
        above = pltpu.roll(edge[0:8], (6 - 2 * q) % 8, 0) if q != 3 else edge[0:8]
        below = pltpu.roll(edge[8:16], (8 - 2 * q) % 8, 0) if q else edge[8:16]
        tiles.append(jnp.where(sub < 4, below, above))
    return jnp.concatenate(tiles, axis=1)


def filter_kernel(own_ref, near_ref, out_ref, differ_ref):
    for h in range(CH):
        for k in range(2):
            differ_ref[h, k, :, 0:BLK_C] = jnp.zeros((24, BLK_C), jnp.float32)
            differ_ref[h, k, :, WIDE - BLK_C : WIDE] = jnp.zeros((24, BLK_C), jnp.float32)

    def fill(g, carry):
        base = pl.multiple_of(BLK_C + g * COLS, BLK_C)
        for h in range(CH):
            part = 2 * g + h
            own = own_ref[part].astype(jnp.float32)
            for k in range(2):
                differ = own - near_ref[2 * part + k].astype(jnp.float32)
                differ_ref[h, k, 0:16, pl.ds(base, COLS)] = differ[:, 0:COLS]
                differ_ref[h, k, 16:24, pl.ds(base, COLS)] = unpack_edge(differ[:, COLS:])
        return carry

    lax.fori_loop(0, SWATHS, fill, 0)

    wide = COLS + 2 * BLK_C

    def step(g, carry):
        base = pl.multiple_of(g * COLS, COLS)
        for h in range(CH):
            lowest = None
            for k in range(2):
                window = differ_ref[h, k, :, pl.ds(base, wide)]
                cols = {}
                for t in (-2, -1, 1, 2):
                    cols[t] = pltpu.roll(window, (-t) % wide, 1)[:, BLK_C : BLK_C + COLS]
                middle = window[:, BLK_C : BLK_C + COLS]

                def row(value, t):
                    return pltpu.roll(value, (-t) % 24, 0)[0:16]

                def combine(m2, m1, p1, p2):
                    return middle[0:16] + 0.25 * (m1 + p1) - 0.5 * (m2 + p2)

                found = [
                    combine(*[cols[t][0:16] for t in (-2, -1, 1, 2)]),
                    combine(*[row(middle, t) for t in (-2, -1, 1, 2)]),
                    combine(*[row(cols[t], t) for t in (-2, -1, 1, 2)]),
                    combine(*[row(cols[-t], t) for t in (-2, -1, 1, 2)]),
                ]
                lowest = found if lowest is None else [jnp.minimum(a, b) for a, b in zip(lowest, found)]
            for d in range(4):
                out_ref[d, g, :, h * COLS : (h + 1) * COLS] = lowest[d].astype(jnp.bfloat16)
        return carry

    lax.fori_loop(0, SWATHS, step, 0)


VMEM = pl.BlockSpec(memory_space=pltpu.VMEM)
SMEM = pl.BlockSpec(memory_space=pltpu.SMEM)
PARAMS = pltpu.CompilerParams(vmem_limit_bytes=VMEM_LIMIT)


def pack(pixels, classes, interpret=False):
    return pl.pallas_call(
        pack_kernel,
        out_shape=jax.ShapeDtypeStruct((SWATHS, BAND, 3 * COLS), jnp.bfloat16),
        in_specs=[VMEM, VMEM],
        out_specs=VMEM,
        scratch_shapes=[pltpu.VMEM((8, COLS), jnp.float32)],
        compiler_params=PARAMS,
        interpret=interpret,
    )(pixels, classes)


def norm(recv, stencils, band=None, interpret=False):
    return pl.pallas_call(
        functools.partial(norm_kernel, band),
        out_shape=jax.ShapeDtypeStruct((PARTS, BAND, PIECE), jnp.bfloat16),
        in_specs=[VMEM, SMEM],
        out_specs=VMEM,
        scratch_shapes=[
            pltpu.VMEM((CH, 24, WIDE), jnp.float32),
            pltpu.VMEM((24, BLK_C), jnp.int32),
            pltpu.SMEM((24, BLK_C), jnp.int32),
            pltpu.SemaphoreType.DMA,
        ],
        compiler_params=PARAMS,
        interpret=interpret,
    )(recv, stencils)


def pick(near, recv, band=None, interpret=False):
    return pl.pallas_call(
        functools.partial(pick_kernel, band),
        out_shape=jax.ShapeDtypeStruct((2 * DIES, BAND, PIECE), jnp.bfloat16),
        in_specs=[SMEM, VMEM],
        out_specs=VMEM,
        compiler_params=PARAMS,
        interpret=interpret,
    )(near, recv)


def filters(own, near, interpret=False):
    return pl.pallas_call(
        filter_kernel,
        out_shape=jax.ShapeDtypeStruct((4, SWATHS, BAND, CH * COLS), jnp.bfloat16),
        in_specs=[VMEM, VMEM],
        out_specs=VMEM,
        scratch_shapes=[pltpu.VMEM((CH, 2, 24, WIDE), jnp.float32)],
        compiler_params=PARAMS,
        interpret=interpret,
    )(own, near)


def shards(swath_pixels, stencils, classes, neighbours):
    near = lax.all_gather(neighbours.reshape(-1), "seg", axis=0, tiled=True)
    packed = pack(swath_pixels[0, 0], classes[0])
    bands = lax.all_to_all(packed, "swath", split_axis=0, concat_axis=0, tiled=True)
    own = norm(bands, stencils.reshape(-1))
    pieces = lax.all_to_all(own, "seg", split_axis=0, concat_axis=0, tiled=True)
    picked = pick(near, pieces)
    references = lax.all_to_all(picked, "seg", split_axis=0, concat_axis=0, tiled=True)
    return filters(own, references)[None]


def solution(mesh):
    return jax.shard_map(
        shards,
        mesh=mesh,
        in_specs=(
            P("swath", "seg", None, None),
            P(),
            P("seg", "swath", None),
            P("seg", None, None),
        ),
        out_specs=P("seg", None, None, "swath", None),
        check_vma=False,
    )
```

```python
import functools

import jax
import jax.numpy as jnp
from jax import lax
from jax.experimental import pallas as pl
from jax.experimental.pallas import tpu as pltpu
from jax.sharding import PartitionSpec as P

CH = 2
BLK_R = 8
BLK_C = 128
NCLASS = 8
SWATHS = 8
DIES = 16
ROWS = 128
COLS = 512
BAND = 16
PARTS = 16
COL_BLOCKS = SWATHS * COLS // BLK_C
WIDE = SWATHS * COLS + 2 * BLK_C
PIECE = COLS + BLK_C
SENT = PIECE + BLK_C
VMEM_LIMIT = 24 * 1024 * 1024

TAPS = (-0.5, 0.25, 1.0, 0.25, -0.5)


def rows_of(count, width):
    return lax.broadcasted_iota(jnp.int32, (count, width), 0)


def pack_kernel(pix_ref, cls_ref, out_ref, row_ref):
    row_ref[...] = jnp.zeros_like(row_ref)
    row_ref[6:8, 0:COL_BLOCKS] = cls_ref[...].astype(jnp.float32)
    own_classes = row_ref[...]
    sub = rows_of(8, COLS)
    for band in range(SWATHS):
        start = band * BAND
        out_ref[band, :, 0 : CH * COLS] = pix_ref[start : start + BAND, :]
        for h in range(CH):
            lanes = slice(h * COLS, (h + 1) * COLS)
            if band > 0:
                above = pix_ref[start - BAND : start, lanes].astype(jnp.float32)[8:16]
                above = pltpu.roll(above, 3, 0)
            else:
                above = jnp.zeros((8, COLS), jnp.float32)
            if band < SWATHS - 1:
                below = pix_ref[start + BAND : start + 2 * BAND, lanes].astype(jnp.float32)[0:8]
                below = pltpu.roll(below, 3, 0)
            else:
                below = jnp.zeros((8, COLS), jnp.float32)
            halo = jnp.where(sub < 3, above, jnp.where(sub < 6, below, own_classes))
            if h == 0:
                first = halo
        out_ref[band, :, CH * COLS :] = jnp.concatenate([first, halo], axis=0).astype(jnp.bfloat16)


def near_tile(band, near_ref):
    blocks = ROWS // BLK_R
    lane = lax.broadcasted_iota(jnp.int32, (16, BLK_C), 1)
    tile = jnp.zeros((16, BLK_C), jnp.int32)
    for i in range(4):
        block = jnp.clip(2 * band - 1 + i, 0, blocks - 1)
        for k in range(2):
            tile = jnp.where(lane == 2 * i + k, near_ref[k, block], tile)
    return tile.astype(jnp.float32)


def norm_kernel(band, recv_ref, sten_ref, near_ref, out_ref, image_ref, cls_v, cls_s, sem):
    if band is None:
        band = lax.axis_index("swath")
    before = jnp.maximum(band - 1, 0)
    after = jnp.minimum(band + 1, SWATHS - 1)

    def class_rows(source):
        return recv_ref[source, :, CH * COLS : CH * COLS + BLK_C].astype(jnp.float32)[0:8].astype(jnp.int32)

    cls_v[0:8] = class_rows(before)
    cls_v[8:16] = class_rows(band)
    cls_v[16:24] = class_rows(after)
    copy = pltpu.make_async_copy(cls_v, cls_s, sem)
    copy.start()

    for h in range(CH):
        image_ref[h, :, 0:BLK_C] = jnp.zeros((24, BLK_C), jnp.float32)
        image_ref[h, :, WIDE - BLK_C : WIDE] = jnp.zeros((24, BLK_C), jnp.float32)
        for g in range(SWATHS):
            lanes = slice(BLK_C + g * COLS, BLK_C + (g + 1) * COLS)
            image_ref[h, 0:16, lanes] = recv_ref[g, :, h * COLS : (h + 1) * COLS].astype(jnp.float32)
            halo = recv_ref[g, :, CH * COLS :].astype(jnp.float32)[h * 8 : h * 8 + 8]
            image_ref[h, 16:24, lanes] = pltpu.roll(halo, 5, 0)
    near = near_tile(band, near_ref).astype(jnp.bfloat16)
    copy.wait()

    top = jnp.where(band > 0, 1.0, 0.0)
    bottom = jnp.where(band < SWATHS - 1, 1.0, 0.0)
    sub = rows_of(8, BLK_C)

    def step(g, carry):
        for h in range(CH):
            base = pl.multiple_of(g * COLS, COLS)
            window = image_ref[h, :, pl.ds(base, COLS + 2 * BLK_C)]
            wide = COLS + 2 * BLK_C
            cols = [
                pltpu.roll(window, 1, 1)[:, BLK_C : BLK_C + COLS],
                window[:, BLK_C : BLK_C + COLS],
                pltpu.roll(window, wide - 1, 1)[:, BLK_C : BLK_C + COLS],
            ]
            shifted = [[pltpu.roll(c, 1, 0), c, pltpu.roll(c, 23, 0)] for c in cols]
            above = jnp.zeros((8, BLK_C), jnp.float32)
            below = jnp.zeros((8, BLK_C), jnp.float32)
            for q in range(COLS // BLK_C):
                block = g * (COLS // BLK_C) + q
                kinds = [cls_s[row, block] for row in (7, 14, 15, 22)]
                total = [jnp.zeros((8, BLK_C), jnp.float32) for _ in range(3)]
                lanes = slice(q * BLK_C, (q + 1) * BLK_C)
                for dr in range(3):
                    for dc in range(3):
                        k = 3 * dr + dc
                        coefs = [sten_ref[kind, h, k] for kind in kinds]
                        source = shifted[dc][dr]
                        edge = jnp.where(sub < 4, coefs[3] * bottom, coefs[0] * top)
                        total[0] = total[0] + coefs[1] * source[0:8, lanes]
                        total[1] = total[1] + coefs[2] * source[8:16, lanes]
                        total[2] = total[2] + edge * source[16:24, lanes]
                out_ref[2 * g + h, :, lanes] = jnp.concatenate(total[:2], axis=0).astype(jnp.bfloat16)
                mine = (sub // 2) == q
                above = jnp.where(mine, pltpu.roll(total[2], (2 * q + 2) % 8, 0), above)
                below = jnp.where(mine, pltpu.roll(total[2], 2 * q, 0) if q else total[2], below)
            out_ref[2 * g + h, :, COLS:PIECE] = jnp.concatenate([above, below], axis=0).astype(jnp.bfloat16)
            out_ref[2 * g + h, :, PIECE:] = near
        return carry

    lax.fori_loop(0, SWATHS, step, 0)


def pick_kernel(recv_ref, out_ref, near_v, near_s, sem):
    sub = rows_of(16, BLK_C)
    near = jnp.zeros((16, BLK_C), jnp.float32)
    for die in range(DIES):
        near = jnp.where(sub == die, recv_ref[die, :, PIECE:].astype(jnp.float32), near)
    near_v[...] = near.astype(jnp.int32)
    copy = pltpu.make_async_copy(near_v, near_s, sem)
    copy.start()
    copy.wait()
    main_top = rows_of(16, COLS) < 8
    edge_top = sub < 8
    for die in range(DIES):
        for k in range(2):
            up, one, two, down = [near_s[die, 2 * i + k] for i in range(4)]
            out_ref[2 * die + k, :, 0:COLS] = jnp.where(
                main_top, recv_ref[one, :, 0:COLS], recv_ref[two, :, 0:COLS]
            )
            out_ref[2 * die + k, :, COLS:] = jnp.where(
                edge_top, recv_ref[up, :, COLS:PIECE], recv_ref[down, :, COLS:PIECE]
            )


def unpack_edge(edge):
    sub = rows_of(8, BLK_C)
    tiles = []
    for q in range(COLS // BLK_C):
        above = pltpu.roll(edge[0:8], (6 - 2 * q) % 8, 0) if q != 3 else edge[0:8]
        below = pltpu.roll(edge[8:16], (8 - 2 * q) % 8, 0) if q else edge[8:16]
        tiles.append(jnp.where(sub < 4, below, above))
    return jnp.concatenate(tiles, axis=1)


def filter_kernel(own_ref, near_ref, out_ref, differ_ref, done_ref, sems):
    for h in range(CH):
        for k in range(2):
            differ_ref[h, k, :, 0:BLK_C] = jnp.zeros((24, BLK_C), jnp.float32)
            differ_ref[h, k, :, WIDE - BLK_C : WIDE] = jnp.zeros((24, BLK_C), jnp.float32)

    def fill(g, carry):
        base = pl.multiple_of(BLK_C + g * COLS, BLK_C)
        for h in range(CH):
            part = 2 * g + h
            own = own_ref[part, :, 0:PIECE].astype(jnp.float32)
            for k in range(2):
                differ = own - near_ref[2 * part + k].astype(jnp.float32)
                differ_ref[h, k, 0:16, pl.ds(base, COLS)] = differ[:, 0:COLS]
                differ_ref[h, k, 16:24, pl.ds(base, COLS)] = unpack_edge(differ[:, COLS:])
        return carry

    lax.fori_loop(0, SWATHS, fill, 0)

    wide = COLS + 2 * BLK_C

    def step(g, carry):
        base = pl.multiple_of(g * COLS, COLS)
        for h in range(CH):
            lowest = None
            for k in range(2):
                window = differ_ref[h, k, :, pl.ds(base, wide)]
                cols = {}
                for t in (-2, -1, 1, 2):
                    cols[t] = pltpu.roll(window, (-t) % wide, 1)[:, BLK_C : BLK_C + COLS]
                middle = window[:, BLK_C : BLK_C + COLS]

                def row(value, t):
                    return pltpu.roll(value, (-t) % 24, 0)[0:16]

                def combine(m2, m1, p1, p2):
                    return middle[0:16] + 0.25 * (m1 + p1) - 0.5 * (m2 + p2)

                found = [
                    combine(*[cols[t][0:16] for t in (-2, -1, 1, 2)]),
                    combine(*[row(middle, t) for t in (-2, -1, 1, 2)]),
                    combine(*[row(cols[t], t) for t in (-2, -1, 1, 2)]),
                    combine(*[row(cols[-t], t) for t in (-2, -1, 1, 2)]),
                ]
                lowest = found if lowest is None else [jnp.minimum(a, b) for a, b in zip(lowest, found)]
            for d in range(4):
                done_ref[g, d, :, h * COLS : (h + 1) * COLS] = lowest[d].astype(jnp.bfloat16)
        pltpu.make_async_copy(done_ref.at[g], out_ref.at[:, g], sems.at[g]).start()
        return carry

    lax.fori_loop(0, SWATHS, step, 0)
    for g in range(SWATHS):
        pltpu.make_async_copy(done_ref.at[g], out_ref.at[:, g], sems.at[g]).wait()


VMEM = pl.BlockSpec(memory_space=pltpu.VMEM)
SMEM = pl.BlockSpec(memory_space=pltpu.SMEM)
PARAMS = pltpu.CompilerParams(vmem_limit_bytes=VMEM_LIMIT)


def pack(pixels, classes, interpret=False):
    return pl.pallas_call(
        pack_kernel,
        out_shape=jax.ShapeDtypeStruct((SWATHS, BAND, 3 * COLS), jnp.bfloat16),
        in_specs=[VMEM, VMEM],
        out_specs=VMEM,
        scratch_shapes=[pltpu.VMEM((8, COLS), jnp.float32)],
        compiler_params=PARAMS,
        interpret=interpret,
    )(pixels, classes)


def norm(recv, stencils, near, band=None, interpret=False):
    return pl.pallas_call(
        functools.partial(norm_kernel, band),
        out_shape=jax.ShapeDtypeStruct((PARTS, BAND, SENT), jnp.bfloat16),
        in_specs=[VMEM, SMEM, SMEM],
        out_specs=VMEM,
        scratch_shapes=[
            pltpu.VMEM((CH, 24, WIDE), jnp.float32),
            pltpu.VMEM((24, BLK_C), jnp.int32),
            pltpu.SMEM((24, BLK_C), jnp.int32),
            pltpu.SemaphoreType.DMA,
        ],
        compiler_params=PARAMS,
        interpret=interpret,
    )(recv, stencils, near)


def pick(recv, interpret=False):
    return pl.pallas_call(
        pick_kernel,
        out_shape=jax.ShapeDtypeStruct((2 * DIES, BAND, PIECE), jnp.bfloat16),
        in_specs=[VMEM],
        out_specs=VMEM,
        scratch_shapes=[
            pltpu.VMEM((16, BLK_C), jnp.int32),
            pltpu.SMEM((16, BLK_C), jnp.int32),
            pltpu.SemaphoreType.DMA,
        ],
        compiler_params=PARAMS,
        interpret=interpret,
    )(recv)


def filters(own, near, interpret=False):
    return pl.pallas_call(
        filter_kernel,
        out_shape=jax.ShapeDtypeStruct((4, SWATHS, BAND, CH * COLS), jnp.bfloat16),
        in_specs=[VMEM, VMEM],
        out_specs=pl.BlockSpec(memory_space=pl.ANY),
        scratch_shapes=[
            pltpu.VMEM((CH, 2, 24, WIDE), jnp.float32),
            pltpu.VMEM((SWATHS, 4, BAND, CH * COLS), jnp.bfloat16),
            pltpu.SemaphoreType.DMA((SWATHS,)),
        ],
        compiler_params=PARAMS,
        interpret=interpret,
    )(own, near)


def shards(swath_pixels, stencils, classes, neighbours):
    packed = pack(swath_pixels[0, 0], classes[0])
    bands = lax.all_to_all(packed, "swath", split_axis=0, concat_axis=0, tiled=True)
    own = norm(bands, stencils, neighbours[0].T)
    pieces = lax.all_to_all(own, "seg", split_axis=0, concat_axis=0, tiled=True)
    picked = pick(pieces)
    references = lax.all_to_all(picked, "seg", split_axis=0, concat_axis=0, tiled=True)
    return filters(own, references)[None]


def solution(mesh):
    return jax.shard_map(
        shards,
        mesh=mesh,
        in_specs=(
            P("swath", "seg", None, None),
            P(),
            P("seg", "swath", None),
            P("seg", None, None),
        ),
        out_specs=P("seg", None, None, "swath", None),
        check_vma=False,
    )
```

```python
import functools

import jax
import jax.numpy as jnp
from jax import lax
from jax.experimental import pallas as pl
from jax.experimental.pallas import tpu as pltpu
from jax.sharding import PartitionSpec as P

CH = 2
BLK_R = 8
BLK_C = 128
NCLASS = 8
SWATHS = 8
DIES = 16
ROWS = 128
COLS = 512
BAND = 16
PARTS = 16
COL_BLOCKS = SWATHS * COLS // BLK_C
QUADS = COLS // BLK_C
TILES = SWATHS * QUADS + 2
PIECE = COLS + BLK_C
SENT = PIECE + BLK_C
VMEM_LIMIT = 32 * 1024 * 1024

TAPS = (-0.5, 0.25, 1.0, 0.25, -0.5)
DIRECTIONS = ((0, 1), (1, 0), (1, 1), (1, -1))


def rows_of(count, width):
    return lax.broadcasted_iota(jnp.int32, (count, width), 0)


def pack_kernel(band, pix_ref, cls_ref, ids_ref, out_ref, near_ref, row_ref):
    if band is None:
        band = lax.axis_index("swath")
    row_ref[...] = jnp.zeros_like(row_ref)
    row_ref[0:2, 0 : ROWS // BLK_R] = ids_ref[...].astype(jnp.float32)
    ids = pltpu.roll(row_ref[:, 0:BLK_C], (BLK_C + 1 - 2 * band) % BLK_C, 1)
    near_ref[...] = jnp.concatenate([ids, jnp.zeros_like(ids)], axis=0).astype(jnp.bfloat16)

    row_ref[...] = jnp.zeros_like(row_ref)
    row_ref[6:8, 0:COL_BLOCKS] = cls_ref[...].astype(jnp.float32)
    own_classes = row_ref[...]
    sub = rows_of(8, COLS)
    for piece in range(SWATHS):
        start = piece * BAND
        out_ref[piece, :, 0 : CH * COLS] = pix_ref[start : start + BAND, :]
        halves = []
        for h in range(CH):
            lanes = slice(h * COLS, (h + 1) * COLS)
            above = jnp.zeros((8, COLS), jnp.float32)
            below = jnp.zeros((8, COLS), jnp.float32)
            if piece > 0:
                above = pltpu.roll(pix_ref[start - BAND : start, lanes].astype(jnp.float32)[8:16], 3, 0)
            if piece < SWATHS - 1:
                below = pltpu.roll(pix_ref[start + BAND : start + 2 * BAND, lanes].astype(jnp.float32)[0:8], 3, 0)
            halves.append(jnp.where(sub < 3, above, jnp.where(sub < 6, below, own_classes)))
        out_ref[piece, :, CH * COLS :] = jnp.concatenate(halves, axis=0).astype(jnp.bfloat16)


def window_of(ref, h, g):
    return jnp.concatenate([ref[h, QUADS * g + q, 0:24] for q in range(QUADS + 2)], axis=1)


def store_shifted(ref, h, g, window, shift):
    width = (QUADS + 2) * BLK_C
    moved = pltpu.roll(window, (-shift) % width, 1)
    for q in range(QUADS):
        value = moved[:, (q + 1) * BLK_C : (q + 2) * BLK_C]
        ref[h, QUADS * g + q + 1, 0:24] = value
        ref[h, QUADS * g + q + 1, 24:32] = value[0:8]


def store_ring(ref, h, tile, rows, halo):
    ref[h, tile, 0:8] = halo
    ref[h, tile, 8:24] = rows
    ref[h, tile, 24:32] = halo


def norm_kernel(
    band, recv_ref, sten_ref, near_ref, out_ref, left_ref, image_ref, right_ref, table_ref, cls_v, cls_s, sem
):
    if band is None:
        band = lax.axis_index("swath")
    before = jnp.maximum(band - 1, 0)
    after = jnp.minimum(band + 1, SWATHS - 1)

    def class_rows(source):
        return recv_ref[source, :, CH * COLS : CH * COLS + BLK_C].astype(jnp.float32)[0:8].astype(jnp.int32)

    cls_v[0:8] = class_rows(before)
    cls_v[8:16] = class_rows(band)
    cls_v[16:24] = class_rows(after)
    copy = pltpu.make_async_copy(cls_v, cls_s, sem)
    copy.start()

    for k in range(CH * 9):
        table_ref[NCLASS, k] = jnp.zeros((8, BLK_C), jnp.float32)
    for kind in range(NCLASS):
        for h in range(CH):
            row = sten_ref[kind, h : h + 1, :]
            for k in range(9):
                table_ref[kind, CH * k + h] = jnp.broadcast_to(row[:, k : k + 1], (8, BLK_C))

    near = near_ref[...]
    sub = rows_of(8, BLK_C)
    for h in range(CH):
        image_ref[h, 0] = jnp.zeros((32, BLK_C), jnp.float32)
        image_ref[h, TILES - 1] = jnp.zeros((32, BLK_C), jnp.float32)
    for g in range(SWATHS):
        for h in range(CH):
            halo = pltpu.roll(recv_ref[g, :, CH * COLS :].astype(jnp.float32)[h * 8 : h * 8 + 8], 5, 0)
            for q in range(QUADS):
                lanes = slice(h * COLS + q * BLK_C, h * COLS + (q + 1) * BLK_C)
                rows = recv_ref[g, :, lanes].astype(jnp.float32)
                store_ring(image_ref, h, QUADS * g + q + 1, rows, halo[:, q * BLK_C : (q + 1) * BLK_C])

    def shift(g):
        for h in range(CH):
            window = window_of(image_ref, h, g)
            store_shifted(left_ref, h, g, window, -1)
            store_shifted(right_ref, h, g, window, 1)

    def step(g):
        for h in range(CH):
            above = jnp.zeros((8, BLK_C), jnp.float32)
            below = jnp.zeros((8, BLK_C), jnp.float32)
            for q in range(QUADS):
                block = g * QUADS + q
                tile = block + 1
                kinds = [cls_s[row, block] for row in (7, 14, 15, 22)]
                kinds[0] = jnp.where(band > 0, kinds[0], NCLASS)
                kinds[3] = jnp.where(band < SWATHS - 1, kinds[3], NCLASS)
                total = [None] * 3
                for dr in range(3):
                    for dc, source in enumerate((left_ref, image_ref, right_ref)):
                        coefs = [table_ref[kind, CH * (3 * dr + dc) + h] for kind in kinds]
                        rows = source[h, tile, pl.ds(7 + dr, BAND)]
                        halo = source[h, tile, pl.ds((23, 0, 1)[dr], 8)]
                        terms = [
                            coefs[1] * rows[0:8],
                            coefs[2] * rows[8:16],
                            jnp.where(sub < 4, coefs[3], coefs[0]) * halo,
                        ]
                        total = [t if s is None else s + t for s, t in zip(total, terms)]
                lanes = slice(q * BLK_C, (q + 1) * BLK_C)
                out_ref[2 * g + h, :, lanes] = jnp.concatenate(total[:2], axis=0).astype(jnp.bfloat16)
                mine = (sub // 2) == q
                above = jnp.where(mine, pltpu.roll(total[2], (2 * q + 2) % 8, 0) if q != 3 else total[2], above)
                below = jnp.where(mine, pltpu.roll(total[2], 2 * q, 0) if q else total[2], below)
            out_ref[2 * g + h, :, COLS:PIECE] = jnp.concatenate([above, below], axis=0).astype(jnp.bfloat16)
            out_ref[2 * g + h, :, PIECE:] = near

    shift(0)
    shift(1)
    copy.wait()
    for g in range(SWATHS):
        if g + 2 < SWATHS:
            shift(g + 2)
        step(g)


def pick_kernel(recv_ref, out_ref, near_v, near_s, sem):
    sub = rows_of(2 * DIES, BLK_C)
    for part in range(DIES // 4):
        ids = jnp.zeros((8, BLK_C), jnp.float32)
        for i in range(4):
            rows = recv_ref[4 * part + i, :, PIECE:].astype(jnp.float32)[0:8]
            ids = jnp.where(sub[0:8] // 2 == i, pltpu.roll(rows, 2 * i, 0) if i else rows, ids)
        near_v[8 * part : 8 * part + 8] = ids.astype(jnp.int32)
    copy = pltpu.make_async_copy(near_v, near_s, sem)
    copy.start()
    copy.wait()
    main_top = rows_of(16, COLS) < 8
    edge_top = sub[0:16] < 8
    for die in range(DIES):
        for k in range(2):
            up, one, two, down = [near_s[2 * die + k, i] for i in range(4)]
            out_ref[2 * die + k, :, 0:COLS] = jnp.where(
                main_top, recv_ref[one, :, 0:COLS], recv_ref[two, :, 0:COLS]
            )
            out_ref[2 * die + k, :, COLS:] = jnp.where(
                edge_top, recv_ref[up, :, COLS:PIECE], recv_ref[down, :, COLS:PIECE]
            )


def filter_kernel(own_ref, near_ref, out_ref, *scratch):
    done_ref, sems = scratch[-2:]
    images = [dict(zip(("full", 1, 2, (1, -1), (1, 1), (2, -2), (2, 2)), scratch[7 * k : 7 * k + 7])) for k in range(2)]
    low = rows_of(8, BLK_C) < 4
    for k in range(2):
        for scale in (1, 2):
            for h in range(CH):
                images[k][scale][h, 0] = jnp.zeros((32, BLK_C), jnp.float32)
                images[k][scale][h, TILES - 1] = jnp.zeros((32, BLK_C), jnp.float32)

    def fill(g):
        for h in range(CH):
            part = 2 * g + h
            own = own_ref[part, :, 0:PIECE].astype(jnp.float32)
            for k in range(2):
                differ = own - near_ref[2 * part + k].astype(jnp.float32)
                edge = differ[:, COLS:]
                for q in range(QUADS):
                    tile = QUADS * g + q + 1
                    up, down = (6 - 2 * q) % 8, (8 - 2 * q) % 8
                    above = pltpu.roll(edge[0:8], up, 0) if up else edge[0:8]
                    below = pltpu.roll(edge[8:16], down, 0) if down else edge[8:16]
                    halo = jnp.where(low, below, above)
                    rows = differ[:, q * BLK_C : (q + 1) * BLK_C]
                    images[k]["full"][h, tile] = rows
                    store_ring(images[k][1], h, tile, 0.25 * rows, 0.25 * halo)
                    store_ring(images[k][2], h, tile, -0.5 * rows, -0.5 * halo)

    def shift(g):
        for h in range(CH):
            for k in range(2):
                for scale in (1, 2):
                    window = window_of(images[k][scale], h, g)
                    for sign in (-1, 1):
                        store_shifted(images[k][scale, sign * scale], h, g, window, sign * scale)

    def step(g):
        for h in range(CH):
            for q in range(QUADS):
                tile = QUADS * g + q + 1
                lowest = None
                for k in range(2):
                    middle = images[k]["full"][h, tile]
                    found = []
                    for a, b in DIRECTIONS:
                        terms = []
                        for t in (-2, -1, 1, 2):
                            source = images[k][abs(t), b * t] if b else images[k][abs(t)]
                            terms.append(source[h, tile, pl.ds(8 + a * t, BAND)])
                        found.append((middle + (terms[1] + terms[2])) + (terms[0] + terms[3]))
                    lowest = found if lowest is None else [jnp.minimum(a, b) for a, b in zip(lowest, found)]
                lanes = slice(h * COLS + q * BLK_C, h * COLS + (q + 1) * BLK_C)
                for d in range(4):
                    done_ref[g, d, :, lanes] = lowest[d].astype(jnp.bfloat16)

    def send(g):
        return pltpu.make_async_copy(done_ref.at[g], out_ref.at[:, g], sems.at[g])

    fill(0)
    fill(1)
    shift(0)
    for g in range(SWATHS):
        if g + 2 < SWATHS:
            fill(g + 2)
        if g + 1 < SWATHS:
            shift(g + 1)
        step(g)
        send(g).start()
    for g in range(SWATHS):
        send(g).wait()


VMEM = pl.BlockSpec(memory_space=pltpu.VMEM)
PARAMS = pltpu.CompilerParams(vmem_limit_bytes=VMEM_LIMIT)


def pack(pixels, classes, near, band=None, interpret=False):
    return pl.pallas_call(
        functools.partial(pack_kernel, band),
        out_shape=(
            jax.ShapeDtypeStruct((SWATHS, BAND, 3 * COLS), jnp.bfloat16),
            jax.ShapeDtypeStruct((16, BLK_C), jnp.bfloat16),
        ),
        in_specs=[VMEM] * 3,
        out_specs=(VMEM,) * 2,
        scratch_shapes=[pltpu.VMEM((8, COLS), jnp.float32)],
        compiler_params=PARAMS,
        interpret=interpret,
    )(pixels, classes, near)


def norm(recv, stencils, near, band=None, interpret=False):
    image = pltpu.VMEM((CH, TILES, 32, BLK_C), jnp.float32)
    return pl.pallas_call(
        functools.partial(norm_kernel, band),
        out_shape=jax.ShapeDtypeStruct((PARTS, BAND, SENT), jnp.bfloat16),
        in_specs=[VMEM, VMEM, VMEM],
        out_specs=VMEM,
        scratch_shapes=[
            image,
            image,
            image,
            pltpu.VMEM((NCLASS + 1, CH * 9, 8, BLK_C), jnp.float32),
            pltpu.VMEM((24, BLK_C), jnp.int32),
            pltpu.SMEM((24, BLK_C), jnp.int32),
            pltpu.SemaphoreType.DMA,
        ],
        compiler_params=PARAMS,
        interpret=interpret,
    )(recv, stencils, near)


def pick(recv, interpret=False):
    return pl.pallas_call(
        pick_kernel,
        out_shape=jax.ShapeDtypeStruct((2 * DIES, BAND, PIECE), jnp.bfloat16),
        in_specs=[VMEM],
        out_specs=VMEM,
        scratch_shapes=[
            pltpu.VMEM((2 * DIES, BLK_C), jnp.int32),
            pltpu.SMEM((2 * DIES, BLK_C), jnp.int32),
            pltpu.SemaphoreType.DMA,
        ],
        compiler_params=PARAMS,
        interpret=interpret,
    )(recv)


def filters(own, near, interpret=False):
    full = pltpu.VMEM((CH, TILES, BAND, BLK_C), jnp.float32)
    image = pltpu.VMEM((CH, TILES, 32, BLK_C), jnp.float32)
    return pl.pallas_call(
        filter_kernel,
        out_shape=jax.ShapeDtypeStruct((4, SWATHS, BAND, CH * COLS), jnp.bfloat16),
        in_specs=[VMEM, VMEM],
        out_specs=pl.BlockSpec(memory_space=pl.ANY),
        scratch_shapes=[
            *([full] + [image] * 6) * 2,
            pltpu.VMEM((SWATHS, 4, BAND, CH * COLS), jnp.bfloat16),
            pltpu.SemaphoreType.DMA((SWATHS,)),
        ],
        compiler_params=PARAMS,
        interpret=interpret,
    )(own, near)


def shards(swath_pixels, stencils, classes, neighbours):
    packed, near = pack(swath_pixels[0, 0], classes[0], neighbours[0].T)
    bands = lax.all_to_all(packed, "swath", split_axis=0, concat_axis=0, tiled=True)
    own = norm(bands, stencils, near)
    pieces = lax.all_to_all(own, "seg", split_axis=0, concat_axis=0, tiled=True)
    picked = pick(pieces)
    references = lax.all_to_all(picked, "seg", split_axis=0, concat_axis=0, tiled=True)
    return filters(own, references)[None]


def solution(mesh):
    return jax.shard_map(
        shards,
        mesh=mesh,
        in_specs=(
            P("swath", "seg", None, None),
            P(),
            P("seg", "swath", None),
            P("seg", None, None),
        ),
        out_specs=P("seg", None, None, "swath", None),
        check_vma=False,
    )
```

```python
import functools

import jax
import jax.numpy as jnp
from jax import lax
from jax.experimental import pallas as pl
from jax.experimental.pallas import tpu as pltpu
from jax.sharding import PartitionSpec as P

CH = 2
BLK_R = 8
BLK_C = 128
NCLASS = 8
SWATHS = 8
DIES = 16
ROWS = 128
COLS = 512
BAND = 16
PARTS = 16
COL_BLOCKS = SWATHS * COLS // BLK_C
QUADS = COLS // BLK_C
TILES = SWATHS * QUADS + 2
PIECE = COLS + BLK_C
SENT = PIECE + BLK_C
VMEM_LIMIT = 32 * 1024 * 1024

TAPS = (-0.5, 0.25, 1.0, 0.25, -0.5)
DIRECTIONS = ((0, 1), (1, 0), (1, 1), (1, -1))


def rows_of(count, width):
    return lax.broadcasted_iota(jnp.int32, (count, width), 0)


def pack_kernel(band, pix_ref, cls_ref, ids_ref, out_ref, near_ref, row_ref):
    if band is None:
        band = lax.axis_index("swath")
    row_ref[...] = jnp.zeros_like(row_ref)
    row_ref[0:2, 0 : ROWS // BLK_R] = ids_ref[...].astype(jnp.float32)
    ids = pltpu.roll(row_ref[:, 0:BLK_C], (BLK_C + 1 - 2 * band) % BLK_C, 1)
    near_ref[...] = jnp.concatenate([ids, jnp.zeros_like(ids)], axis=0).astype(jnp.bfloat16)

    row_ref[...] = jnp.zeros_like(row_ref)
    row_ref[6:8, 0:COL_BLOCKS] = cls_ref[...].astype(jnp.float32)
    own_classes = row_ref[...]
    sub = rows_of(8, COLS)
    for piece in range(SWATHS):
        start = piece * BAND
        out_ref[piece, :, 0 : CH * COLS] = pix_ref[start : start + BAND, :]
        halves = []
        for h in range(CH):
            lanes = slice(h * COLS, (h + 1) * COLS)
            above = jnp.zeros((8, COLS), jnp.float32)
            below = jnp.zeros((8, COLS), jnp.float32)
            if piece > 0:
                above = pltpu.roll(pix_ref[start - BAND : start, lanes].astype(jnp.float32)[8:16], 3, 0)
            if piece < SWATHS - 1:
                below = pltpu.roll(pix_ref[start + BAND : start + 2 * BAND, lanes].astype(jnp.float32)[0:8], 3, 0)
            halves.append(jnp.where(sub < 3, above, jnp.where(sub < 6, below, own_classes)))
        out_ref[piece, :, CH * COLS :] = jnp.concatenate(halves, axis=0).astype(jnp.bfloat16)


def shifter(ref):
    rotated = {}
    lane = lax.broadcasted_iota(jnp.int32, (24, BLK_C), 1)

    def turn(h, tile, shift):
        if tile == 0 or tile == TILES - 1:
            return jnp.zeros((24, BLK_C), jnp.float32)
        if (h, tile, shift) not in rotated:
            rotated[h, tile, shift] = pltpu.roll(ref[h, tile, 0:24], (-shift) % BLK_C, 1)
        return rotated[h, tile, shift]

    def store(target, h, g, shift):
        for tile in range(QUADS * g + 1, QUADS * g + QUADS + 1):
            if shift > 0:
                value = jnp.where(lane < BLK_C - shift, turn(h, tile, shift), turn(h, tile + 1, shift))
            else:
                value = jnp.where(lane < -shift, turn(h, tile - 1, shift), turn(h, tile, shift))
            target[h, tile, 0:24] = value
            target[h, tile, 24:32] = value[0:8]

    return store


def store_ring(ref, h, tile, rows, halo):
    ref[h, tile, 0:8] = halo
    ref[h, tile, 8:24] = rows
    ref[h, tile, 24:32] = halo


def norm_kernel(
    band, recv_ref, sten_ref, near_ref, out_ref, left_ref, image_ref, right_ref, table_ref
):
    if band is None:
        band = lax.axis_index("swath")
    before = jnp.maximum(band - 1, 0)
    after = jnp.minimum(band + 1, SWATHS - 1)

    def class_rows(source):
        return recv_ref[source, :, CH * COLS : CH * COLS + BLK_C].astype(jnp.float32)[0:8].astype(jnp.int32)

    sub = rows_of(8, BLK_C)
    mine = class_rows(band)
    above = jnp.where(band > 0, class_rows(before), NCLASS)
    below = jnp.where(band < SWATHS - 1, class_rows(after), NCLASS)
    above, below = pltpu.roll(above, 1, 0), pltpu.roll(below, 2, 0)
    code = above * 4096 + pltpu.roll(mine, 2, 0) * 256 + pltpu.roll(mine, 1, 0) * 16 + below

    for k in range(CH * 9):
        table_ref[NCLASS, k] = jnp.zeros((8, BLK_C), jnp.float32)
    for kind in range(NCLASS):
        for h in range(CH):
            row = sten_ref[kind, h : h + 1, :]
            for k in range(9):
                table_ref[kind, CH * k + h] = jnp.broadcast_to(row[:, k : k + 1], (8, BLK_C))

    near = near_ref[...]
    shifted = shifter(image_ref)
    for g in range(SWATHS):
        for h in range(CH):
            halo = pltpu.roll(recv_ref[g, :, CH * COLS :].astype(jnp.float32)[h * 8 : h * 8 + 8], 5, 0)
            for q in range(QUADS):
                lanes = slice(h * COLS + q * BLK_C, h * COLS + (q + 1) * BLK_C)
                rows = recv_ref[g, :, lanes].astype(jnp.float32)
                store_ring(image_ref, h, QUADS * g + q + 1, rows, halo[:, q * BLK_C : (q + 1) * BLK_C])

    def shift(g):
        for h in range(CH):
            shifted(left_ref, h, g, -1)
            shifted(right_ref, h, g, 1)

    def step(g):
        for h in range(CH):
            above = jnp.zeros((8, BLK_C), jnp.float32)
            below = jnp.zeros((8, BLK_C), jnp.float32)
            for q in range(QUADS):
                block = g * QUADS + q
                tile = block + 1
                kinds = [(codes[block] >> bits) & 15 for bits in (12, 8, 4, 0)]
                total = [None] * 3
                for dr in range(3):
                    for dc, source in enumerate((left_ref, image_ref, right_ref)):
                        coefs = [table_ref[kind, CH * (3 * dr + dc) + h] for kind in kinds]
                        rows = source[h, tile, pl.ds(7 + dr, BAND)]
                        halo = source[h, tile, pl.ds((23, 0, 1)[dr], 8)]
                        terms = [
                            coefs[1] * rows[0:8],
                            coefs[2] * rows[8:16],
                            jnp.where(sub < 4, coefs[3], coefs[0]) * halo,
                        ]
                        total = [t if s is None else s + t for s, t in zip(total, terms)]
                lanes = slice(q * BLK_C, (q + 1) * BLK_C)
                out_ref[2 * g + h, :, lanes] = jnp.concatenate(total[:2], axis=0).astype(jnp.bfloat16)
                mine = (sub // 2) == q
                above = jnp.where(mine, pltpu.roll(total[2], (2 * q + 2) % 8, 0) if q != 3 else total[2], above)
                below = jnp.where(mine, pltpu.roll(total[2], 2 * q, 0) if q else total[2], below)
            out_ref[2 * g + h, :, COLS:PIECE] = jnp.concatenate([above, below], axis=0).astype(jnp.bfloat16)
            out_ref[2 * g + h, :, PIECE:] = near

    lead = 2
    codes = [code[0, block] for block in range(COL_BLOCKS)]
    for g in range(lead):
        shift(g)
    for g in range(SWATHS):
        if g + lead < SWATHS:
            shift(g + lead)
        step(g)


def pick_kernel(recv_ref, out_ref):
    sub = rows_of(16, BLK_C)
    codes = []
    for part in range(DIES // 4):
        ids = jnp.zeros((8, BLK_C), jnp.float32)
        for i in range(4):
            rows = recv_ref[4 * part + i, :, PIECE:].astype(jnp.float32)[0:8]
            ids = jnp.where(sub[0:8] // 2 == i, pltpu.roll(rows, 2 * i, 0) if i else rows, ids)
        code = ids * 4096.0
        for i, scale in ((1, 256.0), (2, 16.0), (3, 1.0)):
            code = code + scale * pltpu.roll(ids, BLK_C - i, 1)
        codes.append(code.astype(jnp.int32))
    main_top = rows_of(16, COLS) < 8
    edge_top = sub < 8
    for die in range(DIES):
        for k in range(2):
            code = codes[die // 4][2 * (die % 4) + k, 0]
            up, one, two, down = [(code >> bits) & 15 for bits in (12, 8, 4, 0)]
            out_ref[2 * die + k, :, 0:COLS] = jnp.where(
                main_top, recv_ref[one, :, 0:COLS], recv_ref[two, :, 0:COLS]
            )
            out_ref[2 * die + k, :, COLS:] = jnp.where(
                edge_top, recv_ref[up, :, COLS:PIECE], recv_ref[down, :, COLS:PIECE]
            )


def filter_kernel(own_ref, near_ref, out_ref, *scratch):
    done_ref, sems = scratch[-2:]
    images = [dict(zip(("full", 1, 2, (1, -1), (1, 1), (2, -2), (2, 2)), scratch[7 * k : 7 * k + 7])) for k in range(2)]
    low = rows_of(8, BLK_C) < 4
    shifted = [{scale: shifter(images[k][scale]) for scale in (1, 2)} for k in range(2)]

    def fill(g):
        for h in range(CH):
            part = 2 * g + h
            own = own_ref[part, :, 0:PIECE].astype(jnp.float32)
            for k in range(2):
                differ = own - near_ref[2 * part + k].astype(jnp.float32)
                edge = differ[:, COLS:]
                for q in range(QUADS):
                    tile = QUADS * g + q + 1
                    up, down = (6 - 2 * q) % 8, (8 - 2 * q) % 8
                    above = pltpu.roll(edge[0:8], up, 0) if up else edge[0:8]
                    below = pltpu.roll(edge[8:16], down, 0) if down else edge[8:16]
                    halo = jnp.where(low, below, above)
                    rows = differ[:, q * BLK_C : (q + 1) * BLK_C]
                    images[k]["full"][h, tile] = rows
                    store_ring(images[k][1], h, tile, 0.25 * rows, 0.25 * halo)
                    store_ring(images[k][2], h, tile, -0.5 * rows, -0.5 * halo)

    def shift(g):
        for h in range(CH):
            for k in range(2):
                for scale in (1, 2):
                    for sign in (-1, 1):
                        shifted[k][scale](images[k][scale, sign * scale], h, g, sign * scale)

    def step(g):
        for h in range(CH):
            for q in range(QUADS):
                tile = QUADS * g + q + 1
                lowest = None
                for k in range(2):
                    middle = images[k]["full"][h, tile]
                    found = []
                    for a, b in DIRECTIONS:
                        terms = []
                        for t in (-2, -1, 1, 2):
                            source = images[k][abs(t), b * t] if b else images[k][abs(t)]
                            terms.append(source[h, tile, pl.ds(8 + a * t, BAND)])
                        found.append((middle + (terms[1] + terms[2])) + (terms[0] + terms[3]))
                    lowest = found if lowest is None else [jnp.minimum(a, b) for a, b in zip(lowest, found)]
                lanes = slice(h * COLS + q * BLK_C, h * COLS + (q + 1) * BLK_C)
                for d in range(4):
                    done_ref[g, d, :, lanes] = lowest[d].astype(jnp.bfloat16)

    def send(g):
        return pltpu.make_async_copy(done_ref.at[g], out_ref.at[:, g], sems.at[g])

    fill(0)
    fill(1)
    shift(0)
    for g in range(SWATHS):
        if g + 2 < SWATHS:
            fill(g + 2)
        if g + 1 < SWATHS:
            shift(g + 1)
        step(g)
        send(g).start()
    for g in range(SWATHS):
        send(g).wait()


VMEM = pl.BlockSpec(memory_space=pltpu.VMEM)
PARAMS = pltpu.CompilerParams(vmem_limit_bytes=VMEM_LIMIT)


def pack(pixels, classes, near, band=None, interpret=False):
    return pl.pallas_call(
        functools.partial(pack_kernel, band),
        out_shape=(
            jax.ShapeDtypeStruct((SWATHS, BAND, 3 * COLS), jnp.bfloat16),
            jax.ShapeDtypeStruct((16, BLK_C), jnp.bfloat16),
        ),
        in_specs=[VMEM] * 3,
        out_specs=(VMEM,) * 2,
        scratch_shapes=[pltpu.VMEM((8, COLS), jnp.float32)],
        compiler_params=PARAMS,
        interpret=interpret,
    )(pixels, classes, near)


def norm(recv, stencils, near, band=None, interpret=False):
    image = pltpu.VMEM((CH, TILES, 32, BLK_C), jnp.float32)
    return pl.pallas_call(
        functools.partial(norm_kernel, band),
        out_shape=jax.ShapeDtypeStruct((PARTS, BAND, SENT), jnp.bfloat16),
        in_specs=[VMEM, VMEM, VMEM],
        out_specs=VMEM,
        scratch_shapes=[
            image,
            image,
            image,
            pltpu.VMEM((NCLASS + 1, CH * 9, 8, BLK_C), jnp.float32),
        ],
        compiler_params=PARAMS,
        interpret=interpret,
    )(recv, stencils, near)


def pick(recv, interpret=False):
    return pl.pallas_call(
        pick_kernel,
        out_shape=jax.ShapeDtypeStruct((2 * DIES, BAND, PIECE), jnp.bfloat16),
        in_specs=[VMEM],
        out_specs=VMEM,
        compiler_params=PARAMS,
        interpret=interpret,
    )(recv)


def filters(own, near, interpret=False):
    full = pltpu.VMEM((CH, TILES, BAND, BLK_C), jnp.float32)
    image = pltpu.VMEM((CH, TILES, 32, BLK_C), jnp.float32)
    return pl.pallas_call(
        filter_kernel,
        out_shape=jax.ShapeDtypeStruct((4, SWATHS, BAND, CH * COLS), jnp.bfloat16),
        in_specs=[VMEM, VMEM],
        out_specs=pl.BlockSpec(memory_space=pl.ANY),
        scratch_shapes=[
            *([full] + [image] * 6) * 2,
            pltpu.VMEM((SWATHS, 4, BAND, CH * COLS), jnp.bfloat16),
            pltpu.SemaphoreType.DMA((SWATHS,)),
        ],
        compiler_params=PARAMS,
        interpret=interpret,
    )(own, near)


def shards(swath_pixels, stencils, classes, neighbours):
    packed, near = pack(swath_pixels[0, 0], classes[0], neighbours[0].T)
    bands = lax.all_to_all(packed, "swath", split_axis=0, concat_axis=0, tiled=True)
    own = norm(bands, stencils, near)
    pieces = lax.all_to_all(own, "seg", split_axis=0, concat_axis=0, tiled=True)
    picked = pick(pieces)
    references = lax.all_to_all(picked, "seg", split_axis=0, concat_axis=0, tiled=True)
    return filters(own, references)[None]


def solution(mesh):
    return jax.shard_map(
        shards,
        mesh=mesh,
        in_specs=(
            P("swath", "seg", None, None),
            P(),
            P("seg", "swath", None),
            P("seg", None, None),
        ),
        out_specs=P("seg", None, None, "swath", None),
        check_vma=False,
    )
```

```python
import functools

import jax
import jax.numpy as jnp
from jax import lax
from jax.experimental import pallas as pl
from jax.experimental.pallas import tpu as pltpu
from jax.sharding import PartitionSpec as P

CH = 2
BLK_R = 8
BLK_C = 128
NCLASS = 8
SWATHS = 8
CORES = 2
DIES = 16
ROWS = 128
COLS = 512
BAND = 16
PARTS = 16
COL_BLOCKS = SWATHS * COLS // BLK_C
QUADS = COLS // BLK_C
TILES = SWATHS * QUADS + 2
PIECE = COLS + BLK_C
SENT = PIECE + BLK_C
VMEM_LIMIT = 32 * 1024 * 1024

TAPS = (-0.5, 0.25, 1.0, 0.25, -0.5)
DIRECTIONS = ((0, 1), (1, 0), (1, 1), (1, -1))


def rows_of(count, width):
    return lax.broadcasted_iota(jnp.int32, (count, width), 0)


def pack_kernel(band, pix_ref, cls_ref, ids_ref, give_ref, near_ref, *refs):
    keep_refs, row_ref = refs[:-1], refs[-1]
    if band is None:
        band = lax.axis_index("swath")
    row_ref[...] = jnp.zeros_like(row_ref)
    row_ref[0:2, 0 : ROWS // BLK_R] = ids_ref[...].astype(jnp.float32)
    ids = pltpu.roll(row_ref[:, 0:BLK_C], (BLK_C + 1 - 2 * band) % BLK_C, 1)
    near_ref[...] = jnp.concatenate([ids, jnp.zeros_like(ids)], axis=0).astype(jnp.bfloat16)

    row_ref[...] = jnp.zeros_like(row_ref)
    row_ref[6:8, 0:COL_BLOCKS] = cls_ref[...].astype(jnp.float32)
    own_classes = row_ref[...]
    sub = rows_of(8, COLS)
    for turn in range(SWATHS // CORES):
        for other, target in enumerate((keep_refs[turn], give_ref.at[turn])):
            piece = ((band // CORES) ^ turn) * CORES + ((band % CORES) ^ other)
            start = pl.multiple_of(piece * BAND, BAND)
            before = pl.multiple_of(jnp.maximum(piece - 1, 0) * BAND, BAND)
            after = pl.multiple_of(jnp.minimum(piece + 1, SWATHS - 1) * BAND, BAND)
            target[:, 0 : CH * COLS] = pix_ref[pl.ds(start, BAND), :]
            halves = []
            for h in range(CH):
                lanes = slice(h * COLS, (h + 1) * COLS)
                above = pltpu.roll(pix_ref[pl.ds(before, BAND), lanes].astype(jnp.float32)[8:16], 3, 0)
                below = pltpu.roll(pix_ref[pl.ds(after, BAND), lanes].astype(jnp.float32)[0:8], 3, 0)
                above = jnp.where(piece > 0, above, 0.0)
                below = jnp.where(piece < SWATHS - 1, below, 0.0)
                halves.append(jnp.where(sub < 3, above, jnp.where(sub < 6, below, own_classes)))
            target[:, CH * COLS :] = jnp.concatenate(halves, axis=0).astype(jnp.bfloat16)


def part_kernel(got_ref, *out_refs):
    for turn, out_ref in enumerate(out_refs, 1):
        out_ref[...] = got_ref[turn]


def shifter(ref):
    rotated = {}
    lane = lax.broadcasted_iota(jnp.int32, (24, BLK_C), 1)

    def turn(h, tile, shift):
        if tile == 0 or tile == TILES - 1:
            return jnp.zeros((24, BLK_C), jnp.float32)
        if (h, tile, shift) not in rotated:
            rotated[h, tile, shift] = pltpu.roll(ref[h, tile, 0:24], (-shift) % BLK_C, 1)
        return rotated[h, tile, shift]

    def store(target, h, g, shift):
        for tile in range(QUADS * g + 1, QUADS * g + QUADS + 1):
            if shift > 0:
                value = jnp.where(lane < BLK_C - shift, turn(h, tile, shift), turn(h, tile + 1, shift))
            else:
                value = jnp.where(lane < -shift, turn(h, tile - 1, shift), turn(h, tile, shift))
            target[h, tile, 0:24] = value
            target[h, tile, 24:32] = value[0:8]

    return store


def store_ring(ref, h, tile, rows, halo):
    ref[h, tile, 0:8] = halo
    ref[h, tile, 8:24] = rows
    ref[h, tile, 24:32] = halo


def norm_kernel(
    band,
    got_ref,
    keep_ref,
    keep_one,
    keep_two,
    keep_three,
    got_one,
    got_two,
    got_three,
    sten_ref,
    near_ref,
    out_ref,
    left_ref,
    image_ref,
    right_ref,
    table_ref,
    cls_ref,
):
    if band is None:
        band = lax.axis_index("swath")
    before = jnp.maximum(band - 1, 0)
    after = jnp.minimum(band + 1, SWATHS - 1)
    pieces = [(keep_ref, got_ref.at[0]), (keep_one, got_one), (keep_two, got_two), (keep_three, got_three)]
    for turn, pair in enumerate(pieces):
        for other, piece in enumerate(pair):
            source = ((band // CORES) ^ turn) * CORES + ((band % CORES) ^ other)
            edges = piece[:, CH * COLS :].astype(jnp.float32)
            cls_ref[source] = edges[0:8, 0:BLK_C]
            for h in range(CH):
                halo = pltpu.roll(edges[h * 8 : h * 8 + 8], 5, 0)
                for q in range(QUADS):
                    lanes = slice(h * COLS + q * BLK_C, h * COLS + (q + 1) * BLK_C)
                    rows = piece[:, lanes].astype(jnp.float32)
                    store_ring(image_ref, h, QUADS * source + q + 1, rows, halo[:, q * BLK_C : (q + 1) * BLK_C])

    def class_rows(source):
        return cls_ref[source].astype(jnp.int32)

    sub = rows_of(8, BLK_C)
    mine = class_rows(band)
    above = jnp.where(band > 0, class_rows(before), NCLASS)
    below = jnp.where(band < SWATHS - 1, class_rows(after), NCLASS)
    above, below = pltpu.roll(above, 1, 0), pltpu.roll(below, 2, 0)
    code = above * 4096 + pltpu.roll(mine, 2, 0) * 256 + pltpu.roll(mine, 1, 0) * 16 + below

    for k in range(CH * 9):
        table_ref[NCLASS, k] = jnp.zeros((8, BLK_C), jnp.float32)
    for kind in range(NCLASS):
        for h in range(CH):
            row = sten_ref[kind, h : h + 1, :]
            for k in range(9):
                table_ref[kind, CH * k + h] = jnp.broadcast_to(row[:, k : k + 1], (8, BLK_C))

    near = near_ref[...]
    shifted = shifter(image_ref)

    def shift(g):
        for h in range(CH):
            shifted(left_ref, h, g, -1)
            shifted(right_ref, h, g, 1)

    def step(g):
        for h in range(CH):
            above = jnp.zeros((8, BLK_C), jnp.float32)
            below = jnp.zeros((8, BLK_C), jnp.float32)
            for q in range(QUADS):
                block = g * QUADS + q
                tile = block + 1
                kinds = [(codes[block] >> bits) & 15 for bits in (12, 8, 4, 0)]
                total = [None] * 3
                for dr in range(3):
                    for dc, source in enumerate((left_ref, image_ref, right_ref)):
                        coefs = [table_ref[kind, CH * (3 * dr + dc) + h] for kind in kinds]
                        rows = source[h, tile, pl.ds(7 + dr, BAND)]
                        halo = source[h, tile, pl.ds((23, 0, 1)[dr], 8)]
                        terms = [
                            coefs[1] * rows[0:8],
                            coefs[2] * rows[8:16],
                            jnp.where(sub < 4, coefs[3], coefs[0]) * halo,
                        ]
                        total = [t if s is None else s + t for s, t in zip(total, terms)]
                lanes = slice(q * BLK_C, (q + 1) * BLK_C)
                out_ref[2 * g + h, :, lanes] = jnp.concatenate(total[:2], axis=0).astype(jnp.bfloat16)
                mine = (sub // 2) == q
                above = jnp.where(mine, pltpu.roll(total[2], (2 * q + 2) % 8, 0) if q != 3 else total[2], above)
                below = jnp.where(mine, pltpu.roll(total[2], 2 * q, 0) if q else total[2], below)
            out_ref[2 * g + h, :, COLS:PIECE] = jnp.concatenate([above, below], axis=0).astype(jnp.bfloat16)
            out_ref[2 * g + h, :, PIECE:] = near

    lead = 2
    codes = [code[0, block] for block in range(COL_BLOCKS)]
    for g in range(lead):
        shift(g)
    for g in range(SWATHS):
        if g + lead < SWATHS:
            shift(g + lead)
        step(g)


def pick_kernel(recv_ref, out_ref):
    sub = rows_of(16, BLK_C)
    codes = []
    for part in range(DIES // 4):
        ids = jnp.zeros((8, BLK_C), jnp.float32)
        for i in range(4):
            rows = recv_ref[4 * part + i, :, PIECE:].astype(jnp.float32)[0:8]
            ids = jnp.where(sub[0:8] // 2 == i, pltpu.roll(rows, 2 * i, 0) if i else rows, ids)
        code = ids * 4096.0
        for i, scale in ((1, 256.0), (2, 16.0), (3, 1.0)):
            code = code + scale * pltpu.roll(ids, BLK_C - i, 1)
        codes.append(code.astype(jnp.int32))
    main_top = rows_of(16, COLS) < 8
    edge_top = sub < 8
    for die in range(DIES):
        for k in range(2):
            code = codes[die // 4][2 * (die % 4) + k, 0]
            up, one, two, down = [(code >> bits) & 15 for bits in (12, 8, 4, 0)]
            out_ref[2 * die + k, :, 0:COLS] = jnp.where(
                main_top, recv_ref[one, :, 0:COLS], recv_ref[two, :, 0:COLS]
            )
            out_ref[2 * die + k, :, COLS:] = jnp.where(
                edge_top, recv_ref[up, :, COLS:PIECE], recv_ref[down, :, COLS:PIECE]
            )


def filter_kernel(own_ref, near_ref, out_ref, *scratch):
    done_ref, sems = scratch[-2:]
    images = [dict(zip(("full", 1, 2, (1, -1), (1, 1), (2, -2), (2, 2)), scratch[7 * k : 7 * k + 7])) for k in range(2)]
    low = rows_of(8, BLK_C) < 4
    shifted = [{scale: shifter(images[k][scale]) for scale in (1, 2)} for k in range(2)]

    def fill(g):
        for h in range(CH):
            part = 2 * g + h
            own = own_ref[part, :, 0:PIECE].astype(jnp.float32)
            for k in range(2):
                differ = own - near_ref[2 * part + k].astype(jnp.float32)
                edge = differ[:, COLS:]
                for q in range(QUADS):
                    tile = QUADS * g + q + 1
                    up, down = (6 - 2 * q) % 8, (8 - 2 * q) % 8
                    above = pltpu.roll(edge[0:8], up, 0) if up else edge[0:8]
                    below = pltpu.roll(edge[8:16], down, 0) if down else edge[8:16]
                    halo = jnp.where(low, below, above)
                    rows = differ[:, q * BLK_C : (q + 1) * BLK_C]
                    images[k]["full"][h, tile] = rows
                    store_ring(images[k][1], h, tile, 0.25 * rows, 0.25 * halo)
                    store_ring(images[k][2], h, tile, -0.5 * rows, -0.5 * halo)

    def shift(g):
        for h in range(CH):
            for k in range(2):
                for scale in (1, 2):
                    for sign in (-1, 1):
                        shifted[k][scale](images[k][scale, sign * scale], h, g, sign * scale)

    def step(g):
        for h in range(CH):
            for q in range(QUADS):
                tile = QUADS * g + q + 1
                lowest = None
                for k in range(2):
                    middle = images[k]["full"][h, tile]
                    found = []
                    for a, b in DIRECTIONS:
                        terms = []
                        for t in (-2, -1, 1, 2):
                            source = images[k][abs(t), b * t] if b else images[k][abs(t)]
                            terms.append(source[h, tile, pl.ds(8 + a * t, BAND)])
                        found.append((middle + (terms[1] + terms[2])) + (terms[0] + terms[3]))
                    lowest = found if lowest is None else [jnp.minimum(a, b) for a, b in zip(lowest, found)]
                lanes = slice(h * COLS + q * BLK_C, h * COLS + (q + 1) * BLK_C)
                for d in range(4):
                    done_ref[g, d, :, lanes] = lowest[d].astype(jnp.bfloat16)

    def send(g):
        return pltpu.make_async_copy(done_ref.at[g], out_ref.at[:, g], sems.at[g])

    fill(0)
    fill(1)
    shift(0)
    for g in range(SWATHS):
        if g + 2 < SWATHS:
            fill(g + 2)
        if g + 1 < SWATHS:
            shift(g + 1)
        step(g)
        send(g).start()
    for g in range(SWATHS):
        send(g).wait()


VMEM = pl.BlockSpec(memory_space=pltpu.VMEM)
PARAMS = pltpu.CompilerParams(vmem_limit_bytes=VMEM_LIMIT)


PIECES = jax.ShapeDtypeStruct((SWATHS // CORES, BAND, 3 * COLS), jnp.bfloat16)
ONE_PIECE = jax.ShapeDtypeStruct((BAND, 3 * COLS), jnp.bfloat16)


def pack(pixels, classes, near, band=None, interpret=False):
    return pl.pallas_call(
        functools.partial(pack_kernel, band),
        out_shape=(PIECES, jax.ShapeDtypeStruct((16, BLK_C), jnp.bfloat16), *[ONE_PIECE] * 4),
        in_specs=[VMEM] * 3,
        out_specs=(VMEM,) * 6,
        scratch_shapes=[pltpu.VMEM((8, COLS), jnp.float32)],
        compiler_params=PARAMS,
        interpret=interpret,
    )(pixels, classes, near)


def part(got, interpret=False):
    return pl.pallas_call(
        part_kernel,
        out_shape=(ONE_PIECE,) * 3,
        in_specs=[VMEM],
        out_specs=(VMEM,) * 3,
        compiler_params=PARAMS,
        interpret=interpret,
    )(got)


def norm(got, pieces, stencils, near, band=None, interpret=False):
    image = pltpu.VMEM((CH, TILES, 32, BLK_C), jnp.float32)
    return pl.pallas_call(
        functools.partial(norm_kernel, band),
        out_shape=jax.ShapeDtypeStruct((PARTS, BAND, SENT), jnp.bfloat16),
        in_specs=[VMEM] * 10,
        out_specs=VMEM,
        scratch_shapes=[
            image,
            image,
            image,
            pltpu.VMEM((NCLASS + 1, CH * 9, 8, BLK_C), jnp.float32),
            pltpu.VMEM((SWATHS, 8, BLK_C), jnp.float32),
        ],
        compiler_params=PARAMS,
        interpret=interpret,
    )(got, *pieces, stencils, near)


def pick(recv, interpret=False):
    return pl.pallas_call(
        pick_kernel,
        out_shape=jax.ShapeDtypeStruct((2 * DIES, BAND, PIECE), jnp.bfloat16),
        in_specs=[VMEM],
        out_specs=VMEM,
        compiler_params=PARAMS,
        interpret=interpret,
    )(recv)


def filters(own, near, interpret=False):
    full = pltpu.VMEM((CH, TILES, BAND, BLK_C), jnp.float32)
    image = pltpu.VMEM((CH, TILES, 32, BLK_C), jnp.float32)
    return pl.pallas_call(
        filter_kernel,
        out_shape=jax.ShapeDtypeStruct((4, SWATHS, BAND, CH * COLS), jnp.bfloat16),
        in_specs=[VMEM, VMEM],
        out_specs=pl.BlockSpec(memory_space=pl.ANY),
        scratch_shapes=[
            *([full] + [image] * 6) * 2,
            pltpu.VMEM((SWATHS, 4, BAND, CH * COLS), jnp.bfloat16),
            pltpu.SemaphoreType.DMA((SWATHS,)),
        ],
        compiler_params=PARAMS,
        interpret=interpret,
    )(own, near)


def shards(swath_pixels, stencils, classes, neighbours):
    give, near, *keep = pack(swath_pixels[0, 0], classes[0], neighbours[0].T)
    got = lax.ppermute(give, "swath", [(i, i ^ 1) for i in range(SWATHS)])

    def along_y(piece, turn):
        return lax.ppermute(piece, "swath", [(i, i ^ (CORES * turn)) for i in range(SWATHS)])

    moved = [along_y(keep[turn], turn) for turn in range(1, 4)]
    moved += [along_y(piece, turn) for turn, piece in enumerate(part(got), 1)]
    own = norm(got, [keep[0], *moved], stencils, near)
    pieces = lax.all_to_all(own, "seg", split_axis=0, concat_axis=0, tiled=True)
    picked = pick(pieces)
    references = lax.all_to_all(picked, "seg", split_axis=0, concat_axis=0, tiled=True)
    return filters(own, references)[None]


def solution(mesh):
    return jax.shard_map(
        shards,
        mesh=mesh,
        in_specs=(
            P("swath", "seg", None, None),
            P(),
            P("seg", "swath", None),
            P("seg", None, None),
        ),
        out_specs=P("seg", None, None, "swath", None),
        check_vma=False,
    )
```
